32 devices in a mesh: dp: 4 (over y, core), seq: 4 (over z), chan: 2 (over x).
Axes of the slice: x: 2, y: 2, z: 4, core: 2. Of those that a mesh axis runs over, the one named last changes fastest.
Arguments:
- query_rows: bfloat16 [2048, 8192], P(('dp', 'seq'), 'chan'), may hold values from -6 to 6
- key_rows: bfloat16 [2048, 8192], P(('dp', 'seq'), 'chan'), may hold values from -6 to 6
- value_rows: bfloat16 [2048, 8192], P(('dp', 'seq'), 'chan'), may hold values from -6 to 6
- grad_rows: bfloat16 [2048, 8192], P(('dp', 'seq'), 'chan'), may hold values from -6 to 6
- filter_taps: float32 [512, 8192], P(None, ('chan', 'seq')), may hold values from -0.25 to 0.25
Outputs:
- grad_query: bfloat16 [2048, 8192], P(('dp', 'seq'), 'chan')
- grad_key: bfloat16 [2048, 8192], P(('dp', 'seq'), 'chan')
- grad_value: bfloat16 [2048, 8192], P(('dp', 'seq'), 'chan')
- grad_filter: float32 [512, 8192], P('dp', ('chan', 'seq'))
The draws below stay inside these ranges and needn't reach their ends.
All inputs are finite; a program needn't handle non-finite values.
Results may differ from the reference program's by a relative error of at most 0.0059.
Values may be sent and summed in bfloat16 or wider, within the bound.
No kernel may reach another device: no remote copies, remote signals or barrier semaphores. Data moves between devices by JAX's collectives and lax.ppermute only.
A program may use at most 128 MiB of HBM per device.

```python
import jax
import jax.numpy as jnp
from jax import lax

D = 8192
SEQ = 512
TOKENS = 2048
N_DP = 4


def shard_levels(stream_key, dims, cuts, low, high):
    def one(dim, shards_of):
        draws = jax.random.uniform(jax.random.fold_in(jax.random.fold_in(stream_key, 6), dim), (shards_of,), jnp.float32, low / len(cuts), high / len(cuts))
        return jnp.repeat(jnp.exp(draws), dims[dim] // shards_of).reshape((-1,) + (1,) * (len(dims) - dim - 1))

    gain = one(*cuts[0])
    for cut in cuts[1:]:
        gain = gain * one(*cut)
    return gain


def scatter_about(key, dims, width, most, pieces=(), held_as=jnp.bfloat16):
    loudness = shard_levels(key, dims, pieces, -0.22, 0.18) if pieces else 1.0
    values = jax.random.normal(key, dims, jnp.float32) * width * loudness
    return jnp.minimum(jnp.maximum(values, -most), most).astype(held_as)


def setup_inputs(seed: int = 0) -> dict:
    arg_keys = jax.random.split(jax.random.key(seed), 6)
    query_rows = scatter_about(arg_keys[0], (TOKENS, D), 1.0, 6.0, ((0, 16), (1, 2)))
    key_rows = scatter_about(arg_keys[1], (TOKENS, D), 1.0, 6.0, ((0, 16), (1, 2)))
    value_rows = scatter_about(arg_keys[2], (TOKENS, D), 1.0, 6.0, ((0, 16), (1, 2)))
    grad_rows = scatter_about(arg_keys[3], (TOKENS, D), 1.0, 6.0, ((0, 16), (1, 2)))
    filter_taps = scatter_about(arg_keys[4], (SEQ, D), SEQ ** -0.5, 0.25, ((1, 8),), jnp.float32)
    return dict(query_rows=query_rows, key_rows=key_rows, value_rows=value_rows, grad_rows=grad_rows, filter_taps=filter_taps)


def reference(query_rows, key_rows, value_rows, grad_rows, filter_taps):
    mixed = (key_rows.astype(jnp.float32) * value_rows.astype(jnp.float32)).astype(jnp.bfloat16)
    scaled = (grad_rows.astype(jnp.float32) * query_rows.astype(jnp.float32)).astype(jnp.bfloat16)
    spectrum_filter = jnp.fft.rfft(filter_taps.astype(jnp.float32), n=2 * SEQ, axis=0)

    def replica(pair):
        mix_part, scaled_part = pair
        spectrum_mixed = jnp.fft.rfft(mix_part.astype(jnp.float32), n=2 * SEQ, axis=0)
        spectrum_scaled = jnp.fft.rfft(scaled_part.astype(jnp.float32), n=2 * SEQ, axis=0)
        conv_part = jnp.fft.irfft(spectrum_mixed * spectrum_filter, n=2 * SEQ, axis=0)[:SEQ]
        back_part = jnp.fft.irfft(jnp.conj(spectrum_filter) * spectrum_scaled, n=2 * SEQ, axis=0)[:SEQ]
        taps_part = jnp.fft.irfft(jnp.conj(spectrum_mixed) * spectrum_scaled, n=2 * SEQ, axis=0)[:SEQ]
        return conv_part.astype(jnp.bfloat16), back_part.astype(jnp.bfloat16), taps_part.astype(jnp.float32)

    convs, backs, taps = lax.map(replica, (mixed.reshape(N_DP, SEQ, D), scaled.reshape(N_DP, SEQ, D)))
    grad_filter = jnp.sum(taps, axis=0)
    conv = convs.reshape(TOKENS, D).astype(jnp.float32)
    back = backs.reshape(TOKENS, D).astype(jnp.float32)
    grad_query = (grad_rows.astype(jnp.float32) * conv).astype(jnp.bfloat16)
    grad_key = (back * value_rows.astype(jnp.float32)).astype(jnp.bfloat16)
    grad_value = (back * key_rows.astype(jnp.float32)).astype(jnp.bfloat16)
    return grad_query, grad_key, grad_value, grad_filter
```

```python
import functools

import jax
import jax.numpy as jnp
import ml_dtypes
import numpy as np
from jax import lax
from jax.experimental import pallas as pl
from jax.experimental.pallas import tpu as pltpu
from jax.sharding import PartitionSpec as P


def split_bf16(x):
    high = x.astype(ml_dtypes.bfloat16)
    return np.stack([high, (x - high.astype(np.float64)).astype(ml_dtypes.bfloat16)])


@functools.cache
def tables(half_len):
    freq = 2 * np.arange(half_len)[:, None] + 1
    angles = np.pi * (freq * np.arange(half_len)[None, :] % (4 * half_len)) / (2 * half_len)
    forward = np.concatenate([np.cos(angles), -np.sin(angles)], axis=0)
    both = [forward, forward[:, ::-1]]
    return (
        np.stack([split_bf16(m) for m in both]),
        np.stack([split_bf16(m.T / half_len) for m in both]),
    )


def hop(half, across, steps):
    return [
        (h * half + p, (h ^ across) * half + (p + steps) % half)
        for h in (0, 1)
        for p in range(half)
    ]


def flip(size, bit):
    return [(d, d ^ bit) for d in range(size)]


def after(place, steps, half):
    return lax.rem(place + steps, half)


def before(place, steps, half):
    return lax.rem(place + half - steps, half)


def group_of(info, place, other, half):
    side = 1 - info[0] if other else info[0]
    return side * half + place


def gate_kernel(half, info, *refs):
    inputs, outputs = refs[: 8 * half], refs[8 * half :]
    lower = info[0] == 0
    for r in range(half):
        pair, cross = outputs[r], outputs[half + r]
        for t in (0, 1):
            query, key, value, grad = (
                ref[...].astype(jnp.float32) for ref in inputs[8 * r + 4 * t : 8 * r + 4 * t + 4]
            )
            mixed, scaled = key * value, grad * query
            first = jnp.where(lower, mixed, scaled).astype(jnp.bfloat16)
            pair[t] = first
            pair[2 + t] = jnp.where(lower, scaled, mixed).astype(jnp.bfloat16)
            if t == 1:
                cross[...] = first


def gate(info, half, chunk, chunks, rows):
    tokens, channels = rows[0].shape
    width = channels // (2 * half * chunks)
    in_specs = [
        pl.BlockSpec(
            (tokens, width),
            lambda i, info, r=r, t=t: (
                0,
                group_of(info, after(info[1], r, half), t, half) * chunks + chunk,
            ),
        )
        for r in range(half)
        for t in (0, 1)
        for _ in range(4)
    ]
    shapes = [(4, tokens, width)] * half + [(tokens, width)] * half
    outs = pl.pallas_call(
        functools.partial(gate_kernel, half),
        grid_spec=pltpu.PrefetchScalarGridSpec(
            num_scalar_prefetch=1,
            grid=(1,),
            in_specs=in_specs,
            out_specs=[
                pl.BlockSpec(s, lambda i, info, n=len(s): (0,) * n) for s in shapes
            ],
        ),
        out_shape=[jax.ShapeDtypeStruct(s, jnp.bfloat16) for s in shapes],
        compiler_params=pltpu.CompilerParams(vmem_limit_bytes=24 << 20),
        cost_estimate=pl.CostEstimate(
            flops=4 * tokens * channels // chunks,
            bytes_accessed=13 * tokens * channels // chunks,
            transcendentals=0,
        ),
    )(info, *(list(rows) * (2 * half)))
    return outs[:half], outs[half:]


def high_low(x):
    high = x.astype(jnp.bfloat16)
    return high, (x - high.astype(jnp.float32)).astype(jnp.bfloat16)


def dot(a, b):
    return jnp.dot(a, b, preferred_element_type=jnp.float32)


def times(a, b):
    return a[0] * b[0] - a[1] * b[1], a[0] * b[1] + a[1] * b[0]


def conj_times(a, b):
    return a[0] * b[0] + a[1] * b[1], a[0] * b[1] - a[1] * b[0]


def plus(a, b):
    return a[0] + b[0], a[1] + b[1]


def spectral_kernel(half, replicas, info, *refs):
    pairs, crosses = refs[:half], refs[half : 2 * half]
    taps, near, fwd_data, fwd, inv_data, inv = refs[2 * half : 2 * half + 6]
    outs = refs[2 * half + 6 :]
    pair_outs, cross_outs = outs[:half], outs[half : 2 * half]
    keep, send = outs[2 * half : 2 * half + 2]
    data, tap_high, tap_low, spec, tap_spec, high, low, conv, grads = outs[2 * half + 2 :]
    place, replica = info[1], info[2]
    block, width = crosses[0].shape
    length = half * block

    def cols(i, n=1):
        return slice(i * width, (i + n) * width)

    for r in range(half):
        rows = pl.ds(pl.multiple_of(before(place, r, half) * block, block), block)
        for j in range(4):
            data[rows, cols(j)] = pairs[r][j]
        data[rows, cols(4)] = crosses[r][...]
    for j in (0, 1):
        tap_high[:, cols(j)], tap_low[:, cols(j)] = high_low(taps[j * length : (j + 1) * length, :])
    piece = length // replicas
    bits = replicas.bit_length() - 1
    for j in range(replicas):
        mask = sum(((j >> s) & 1) << (bits - 1 - s) for s in range(bits))
        rows = pl.ds(pl.multiple_of((replica ^ mask) * piece, piece), piece)
        tap_high[rows, cols(2)] = near[j * piece : (j + 1) * piece, :]

    spec[...] = dot(fwd_data[0, 0], data[...]) + dot(fwd_data[0, 1], data[...])
    tap_spec[...] = dot(fwd[0, 0], tap_high[...]) + dot(fwd[0, 1], tap_high[...])
    tap_spec[:, cols(0, 2)] += dot(fwd[0, 0], tap_low[...])

    strip = 16
    odd = lax.broadcasted_iota(jnp.int32, (strip, width), 0) % 2
    sign = (1 - 2 * odd).astype(jnp.float32)

    def late(x):
        return sign * x[1], -sign * x[0]

    def early(x):
        return -sign * x[1], sign * x[0]

    def products(i, carry):
        re = pl.ds(pl.multiple_of(i * strip, strip), strip)
        im = pl.ds(pl.multiple_of(length + i * strip, strip), strip)

        def load(ref, j):
            return ref[re, cols(j)], ref[im, cols(j)]

        def store(j, x):
            for rows, part in ((re, x[0]), (im, x[1])):
                high[rows, cols(j)], low[rows, cols(j)] = high_low(part)

        a_own, a_other, c_own, c_other = (load(spec, j) for j in range(4))
        c_far = late(load(spec, 4))
        h_own, h_far, h_other = (load(tap_spec, j) for j in range(3))
        h_all = plus(h_own, late(h_far))
        store(0, times(a_own, h_own))
        store(1, times(a_other, h_other))
        store(2, plus(conj_times(h_own, c_own), conj_times(h_all, c_far)))
        store(3, conj_times(h_other, c_other))
        store(4, early(times(a_own, h_all)))
        store(5, conj_times(a_own, plus(c_own, c_far)))
        store(6, early(conj_times(a_own, c_far)))
        store(7, conj_times(a_other, c_other))
        return carry

    lax.fori_loop(0, length // strip, products, 0)

    def inverse(matrix, span):
        return (
            dot(matrix[0, 0], high[:, span])
            + dot(matrix[0, 0], low[:, span])
            + dot(matrix[0, 1], high[:, span])
        )

    conv[...] = inverse(inv_data, cols(0, 5)).astype(jnp.bfloat16)
    grads[...] = inverse(inv, cols(5, 3))

    for r in range(half):
        rows = pl.ds(pl.multiple_of(after(place, r, half) * block, block), block)
        for j in range(4):
            pair_outs[r][j] = conv[rows, cols(j)]
        cross_outs[r][...] = conv[rows, cols(4)]
    lags = 2 * length // replicas
    for ref, core in ((keep, replica % 2), (send, 1 - replica % 2)):
        for i in range(3 * replicas // 4):
            col, j = divmod(i, replicas // 4)
            rows = pl.ds(pl.multiple_of((2 * j + core) * lags, lags), lags)
            ref[i * lags : (i + 1) * lags, :] = grads[rows, cols(col)]


def spectral(info, half, replicas, chunk, pairs, crosses, taps, near):
    block, width = crosses[0].shape
    length = half * block
    tile = min(256, width)
    steps = width // tile
    forward, inverse = (jnp.asarray(t) for t in tables(length))
    pair_spec = pl.BlockSpec((4, block, tile), lambda i, info: (0, 0, i))
    cross_spec = pl.BlockSpec((block, tile), lambda i, info: (0, i))
    lag_rows = 3 * length // 2

    def table_spec(t, chosen):
        return pl.BlockSpec(
            (1,) + t.shape[1:], lambda i, info: (info[0] if chosen else 0, 0, 0, 0)
        )

    outs = pl.pallas_call(
        functools.partial(spectral_kernel, half, replicas),
        grid_spec=pltpu.PrefetchScalarGridSpec(
            num_scalar_prefetch=1,
            grid=(steps,),
            in_specs=[pair_spec] * half
            + [cross_spec] * half
            + [
                pl.BlockSpec((2 * length, tile), lambda i, info: (0, chunk * steps + i)),
                pl.BlockSpec((length, tile), lambda i, info: (0, chunk * steps + i)),
                table_spec(forward, True),
                table_spec(forward, False),
                table_spec(inverse, True),
                table_spec(inverse, False),
            ],
            out_specs=[pair_spec] * half
            + [cross_spec] * half
            + [pl.BlockSpec((lag_rows, tile), lambda i, info: (0, i))] * 2,
            scratch_shapes=[
                pltpu.VMEM((length, 5 * tile), jnp.bfloat16),
                pltpu.VMEM((length, 3 * tile), jnp.bfloat16),
                pltpu.VMEM((length, 2 * tile), jnp.bfloat16),
                pltpu.VMEM((2 * length, 5 * tile), jnp.float32),
                pltpu.VMEM((2 * length, 3 * tile), jnp.float32),
                pltpu.VMEM((2 * length, 8 * tile), jnp.bfloat16),
                pltpu.VMEM((2 * length, 8 * tile), jnp.bfloat16),
                pltpu.VMEM((length, 5 * tile), jnp.bfloat16),
                pltpu.VMEM((length, 3 * tile), jnp.float32),
            ],
        ),
        out_shape=[jax.ShapeDtypeStruct((4, block, width), jnp.bfloat16)] * half
        + [jax.ShapeDtypeStruct((block, width), jnp.bfloat16)] * half
        + [jax.ShapeDtypeStruct((lag_rows, width), jnp.float32)] * 2,
        compiler_params=pltpu.CompilerParams(vmem_limit_bytes=48 << 20),
        cost_estimate=pl.CostEstimate(
            flops=2 * 42 * 2 * length * length * width,
            bytes_accessed=2 * length * width * 16,
            transcendentals=0,
        ),
    )(info, *pairs, *crosses, taps, near, forward, forward, inverse, inverse)
    return outs[:half], outs[half : 2 * half], outs[2 * half], outs[2 * half + 1]


def finish_kernel(half, chunks, info, *refs):
    received = refs[: 2 * half * chunks]
    grad, value, key, grad_query, grad_key, grad_value = refs[2 * half * chunks :]
    step = pl.program_id(0)
    lower = info[0] == 0
    for s in range(2 * half * chunks):
        chunk, r, t = s // (2 * half), s // 2 % half, s % 2

        @pl.when(step == s)
        def _(chunk=chunk, r=r, t=t):
            pair, cross = received[2 * half * chunk + r], received[2 * half * chunk + half + r]
            first = pair[t].astype(jnp.float32)
            second = pair[2 + t].astype(jnp.float32)
            if t == 1:
                second = (second + cross[...].astype(jnp.float32)).astype(jnp.bfloat16)
                second = second.astype(jnp.float32)
            conv = jnp.where(lower, first, second)
            back = jnp.where(lower, second, first)
            grad_query[...] = (grad[...].astype(jnp.float32) * conv).astype(jnp.bfloat16)
            grad_key[...] = (back * value[...].astype(jnp.float32)).astype(jnp.bfloat16)
            grad_value[...] = (back * key[...].astype(jnp.float32)).astype(jnp.bfloat16)


def finish(info, half, received, grad, value, key):
    chunks = len(received)
    tokens, channels = grad.shape
    width = channels // (2 * half * chunks)

    def column(s, info):
        chunk, r, t = s // (2 * half), s // 2 % half, s % 2
        side = t + info[0] - 2 * t * info[0]
        return 0, (side * half + before(info[1], r, half)) * chunks + chunk

    flat = [x for pairs, crosses in received for x in (*pairs, *crosses)]
    row_spec = pl.BlockSpec((tokens, width), column)
    return pl.pallas_call(
        functools.partial(finish_kernel, half, chunks),
        grid_spec=pltpu.PrefetchScalarGridSpec(
            num_scalar_prefetch=1,
            grid=(2 * half * chunks,),
            in_specs=[
                pl.BlockSpec(x.shape, lambda s, info, n=x.ndim: (0,) * n) for x in flat
            ]
            + [row_spec] * 3,
            out_specs=[row_spec] * 3,
        ),
        out_shape=[jax.ShapeDtypeStruct((tokens, channels), jnp.bfloat16)] * 3,
        compiler_params=pltpu.CompilerParams(vmem_limit_bytes=32 << 20),
        cost_estimate=pl.CostEstimate(
            flops=4 * tokens * channels,
            bytes_accessed=17 * tokens * channels,
            transcendentals=0,
        ),
    )(info, *flat, grad, value, key)


def spread_taps(taps, half, replicas):
    length = taps.shape[0] // 2
    piece = length // replicas
    mine = lax.dynamic_slice_in_dim(taps, lax.axis_index("dp") * piece, piece, 0)
    near = lax.ppermute(mine.astype(jnp.bfloat16), "seq", hop(half, 1, 0))
    bit = replicas // 2
    while bit:
        near = jnp.concatenate([near, lax.ppermute(near, "dp", flip(replicas, bit))], axis=0)
        bit //= 2
    return near


def sum_filter(keeps, sends, half, replicas):
    replica = lax.axis_index("dp")
    lags = 4 * keeps[0].shape[0] // (3 * replicas)
    arrived = [lax.ppermute(x, "dp", flip(replicas, 1)) for x in sends]
    total = jnp.concatenate([a + b for a, b in zip(keeps, arrived, strict=True)], axis=1)
    blocks = total.reshape(-1, lags, total.shape[1])
    own, other = blocks[: replicas // 2], blocks[replicas // 2 :]

    def halve(x, bit, wire):
        upper = replica & bit != 0
        x = x.reshape(-1, 2, *x.shape[1:])
        go = jnp.where(upper, x[:, 0], x[:, 1]).astype(wire)
        stay = jnp.where(upper, x[:, 1], x[:, 0])
        return stay + lax.ppermute(go, "dp", flip(replicas, bit)).astype(jnp.float32)

    bit = 2
    while bit < replicas // 2:
        own, other = halve(own, bit, jnp.float32), halve(other, bit, jnp.float32)
        bit *= 2
    over = lax.ppermute(other[0].astype(jnp.bfloat16), "seq", hop(half, 1, 0))
    own = jnp.stack([own[0] + over.astype(jnp.float32), own[1]])
    return halve(own, bit, jnp.bfloat16)[0]


def local(replicas, half, query, key, value, grad, taps):
    place = lax.axis_index("seq")
    info = jnp.stack([place // half, place % half, lax.axis_index("dp")]).astype(jnp.int32)
    chunks = 2 if taps.shape[1] % 256 == 0 else 1
    near = spread_taps(taps, half, replicas)
    ready = []
    for chunk in range(chunks):
        pairs, crosses = gate(info, half, chunk, chunks, (query, key, value, grad))
        pairs = [lax.ppermute(x, "seq", hop(half, 0, r)) if r else x for r, x in enumerate(pairs)]
        crosses = [lax.ppermute(x, "seq", hop(half, 1, r)) for r, x in enumerate(crosses)]
        ready.append((pairs, crosses))
    received, keeps, sends = [], [], []
    for chunk, (pairs, crosses) in enumerate(ready):
        pairs, crosses, keep, send = spectral(
            info, half, replicas, chunk, pairs, crosses, taps, near
        )
        pairs = [lax.ppermute(x, "seq", hop(half, 0, r)) if r else x for r, x in enumerate(pairs)]
        crosses = [lax.ppermute(x, "seq", hop(half, 1, r)) for r, x in enumerate(crosses)]
        received.append((pairs, crosses))
        keeps.append(keep)
        sends.append(send)
    grad_filter = sum_filter(keeps, sends, half, replicas)
    return *finish(info, half, received, grad, value, key), grad_filter


def solution(mesh):
    rows = P(("dp", "seq"), "chan")
    return jax.shard_map(
        functools.partial(local, mesh.shape["dp"], mesh.shape["seq"] // 2),
        mesh=mesh,
        in_specs=(rows, rows, rows, rows, P(None, ("chan", "seq"))),
        out_specs=(rows, rows, rows, P("dp", ("chan", "seq"))),
        check_vma=False,
    )
```

```python
import functools

import jax
import jax.numpy as jnp
import ml_dtypes
import numpy as np
from jax import lax
from jax.experimental import pallas as pl
from jax.experimental.pallas import tpu as pltpu
from jax.sharding import PartitionSpec as P


def split_bf16(x):
    high = x.astype(ml_dtypes.bfloat16)
    return np.concatenate([high, (x - high.astype(np.float64)).astype(ml_dtypes.bfloat16)])


@functools.cache
def tables(half_len):
    freq = 2 * np.arange(half_len)[:, None] + 1
    angles = np.pi * (freq * np.arange(half_len)[None, :] % (4 * half_len)) / (2 * half_len)
    forward = np.concatenate([np.cos(angles), -np.sin(angles)], axis=0)
    both = [forward, forward[:, ::-1]]
    return (
        np.concatenate([split_bf16(m) for m in both]),
        np.concatenate([(m.T / half_len).astype(ml_dtypes.bfloat16) for m in both]),
    )


VMEM = 12 << 20
tiny = pl.CostEstimate(flops=0, bytes_accessed=1, transcendentals=0)
large = pl.CostEstimate(flops=1 << 35, bytes_accessed=1, transcendentals=0)


def hop(half, across, steps):
    return [
        (h * half + p, (h ^ across) * half + (p + steps) % half)
        for h in (0, 1)
        for p in range(half)
    ]


def flip(size, bit):
    return [(d, d ^ bit) for d in range(size)]


def after(place, steps, half):
    return lax.rem(place + steps, half)


def before(place, steps, half):
    return lax.rem(place + half - steps, half)


def group_of(info, place, other, half):
    side = 1 - info[0] if other else info[0]
    return side * half + place


def gate_kernel(half, spans, info, *refs):
    inputs, taps, outputs = refs[: 8 * half], refs[8 * half], refs[8 * half + 1 :]
    lower = info[0] == 0
    outputs[-1][...] = taps[...].astype(jnp.bfloat16)
    for r in range(half):
        for t in (0, 1):
            query, key, value, grad = (
                ref[...].astype(jnp.float32) for ref in inputs[8 * r + 4 * t : 8 * r + 4 * t + 4]
            )
            mixed, scaled = key * value, grad * query
            first = jnp.where(lower, mixed, scaled).astype(jnp.bfloat16)
            second = jnp.where(lower, scaled, mixed).astype(jnp.bfloat16)
            for chunk, cols in enumerate(spans):
                outputs[chunk * 2 * half + r][t] = first[:, cols]
                outputs[chunk * 2 * half + r][2 + t] = second[:, cols]
                if t:
                    outputs[chunk * 2 * half + half + r][...] = first[:, cols]


def gate(info, half, spans, rows, taps):
    tokens, channels = rows[0].shape
    group = channels // (2 * half)
    piece = taps.shape[0] // 4

    def column(i, info, r, t):
        return (0, group_of(info, after(info[1], r, half), t, half))

    in_specs = [
        pl.BlockSpec((tokens, group), functools.partial(column, r=r, t=t))
        for r in range(half)
        for t in (0, 1)
        for _ in range(4)
    ]
    in_specs.append(pl.BlockSpec((piece, group), lambda i, info: (info[2] % 2, 0)))
    shapes = []
    for cols in spans:
        width = cols.stop - cols.start
        shapes += [(4, tokens, width)] * half + [(tokens, width)] * half
    shapes.append((piece, group))
    outs = pl.pallas_call(
        functools.partial(gate_kernel, half, spans),
        grid_spec=pltpu.PrefetchScalarGridSpec(
            num_scalar_prefetch=1,
            grid=(1,),
            in_specs=in_specs,
            out_specs=[
                pl.BlockSpec(s, lambda i, info, n=len(s): (0,) * n) for s in shapes
            ],
        ),
        out_shape=[jax.ShapeDtypeStruct(s, jnp.bfloat16) for s in shapes],
        compiler_params=pltpu.CompilerParams(vmem_limit_bytes=56 << 20),
        cost_estimate=tiny,
    )(info, *(list(rows) * (2 * half)), taps)
    parts = [outs[2 * half * c : 2 * half * (c + 1)] for c in range(len(spans))]
    return [x[:half] for x in parts], [x[half:] for x in parts], outs[-1]


def high_low(x):
    high = x.astype(jnp.bfloat16)
    return high, (x - high.astype(jnp.float32)).astype(jnp.bfloat16)


def dot(a, b):
    return jnp.dot(a, b, preferred_element_type=jnp.float32)


def times(a, b):
    return a[0] * b[0] - a[1] * b[1], a[0] * b[1] + a[1] * b[0]


def conj_times(a, b):
    return a[0] * b[0] + a[1] * b[1], a[0] * b[1] - a[1] * b[0]


def plus(a, b):
    return a[0] + b[0], a[1] + b[1]


def load(ref, j, re, im, width):
    cols = slice(j * width, (j + 1) * width)
    return ref[re, cols], ref[im, cols]


def store(ref, j, re, im, x):
    width = x[0].shape[1]
    cols = slice(j * width, (j + 1) * width)
    ref[re, cols] = x[0].astype(ref.dtype)
    ref[im, cols] = x[1].astype(ref.dtype)


def by_strips(length, width, body):
    strip = 16
    odd = lax.broadcasted_iota(jnp.int32, (strip, width), 0) % 2
    sign = (1 - 2 * odd).astype(jnp.float32)

    def late(x):
        return sign * x[1], -sign * x[0]

    def early(x):
        return -sign * x[1], sign * x[0]

    def step(i, carry):
        re = pl.ds(pl.multiple_of(i * strip, strip), strip)
        im = pl.ds(pl.multiple_of(length + i * strip, strip), strip)
        body(re, im, late, early)
        return carry

    lax.fori_loop(0, length // strip, step, 0, unroll=4)


def chosen(table, side):
    rows = table.shape[0] // 2
    return table[pl.ds(pl.multiple_of(side * rows, rows), rows), :]


def transform(matrix, x):
    rows = matrix.shape[0] // 2
    return dot(matrix[:rows], x) + dot(matrix[rows:], x)


def place_rows(target, j, sources, cols, place, half):
    block, width = sources[0].shape[0], cols.stop - cols.start
    for r, source in enumerate(sources):
        rows = pl.ds(pl.multiple_of(before(place, r, half) * block, block), block)
        target[rows, j * width : (j + 1) * width] = source[:, cols]


def split_lags(grads, j, keep, cols, send, row, replicas, core):
    lags, width = 2 * grads.shape[0] // replicas, cols.stop - cols.start
    for ref, cols, mine in ((keep, cols, core), (send, slice(0, width), 1 - core)):
        for i in range(replicas // 4):
            rows = pl.ds(pl.multiple_of((2 * i + mine) * lags, lags), lags)
            part = grads[rows, j * width : (j + 1) * width]
            ref[row + i * lags : row + (i + 1) * lags, cols] = part.astype(ref.dtype)


def taps_kernel(tile, info, taps, fwd, near_spec, all_spec, high, low):
    length = taps.shape[0] // 2
    matrix = chosen(fwd, 0)
    for cols in tiles(taps.shape[1], tile):
        for j in (0, 1):
            part = slice(j * tile, (j + 1) * tile)
            high[:, part], low[:, part] = high_low(taps[j * length : (j + 1) * length, cols])
        spec = transform(matrix, high[...]) + dot(matrix[: 2 * length], low[...])
        near_spec[:, cols] = spec[:, :tile]
        all_spec[:, cols] = spec[:, tile:]

        def body(re, im, late, early, cols=cols):
            far = late((all_spec[re, cols], all_spec[im, cols]))
            all_spec[re, cols] = near_spec[re, cols] + far[0]
            all_spec[im, cols] = near_spec[im, cols] + far[1]

        by_strips(length, tile, body)


def conv_kernel(half, replicas, start, tile, info, *refs):
    pairs, crosses, refs = refs[:half], refs[half : 2 * half], refs[2 * half :]
    tap_spec, tap_all, *near, fwd, inv = refs[:6]
    refs = refs[7 if start else 6 :]
    pair_outs, cross_outs, keep = refs[:half], refs[half : 2 * half], refs[2 * half]
    *sends, data, near_all, spec, near_spec, high, conv, grads = refs[2 * half + 1 :]
    side, place, core = info[0], info[1], info[2] % 2
    _, block, width = pairs[0].shape
    length = half * block
    piece = length // 2
    fwd_data, inv_data = chosen(fwd, side), chosen(inv, side)
    for cols, send in zip(tiles(width, tile), sends, strict=True):
        wide = cols.stop - cols.start
        whole = slice(start + cols.start, start + cols.stop)
        for j in range(4):
            place_rows(data, j, [pair.at[j] for pair in pairs], cols, place, half)
        place_rows(data, 4, crosses, cols, place, half)
        for j in (0, 1):
            rows = pl.ds(pl.multiple_of((core ^ j) * piece, piece), piece)
            near_all[rows, :wide] = near[j][:, whole]
        spec[:, : 5 * wide] = transform(fwd_data, data[:, : 5 * wide])
        near_spec[:, :wide] = transform(chosen(fwd, 0), near_all[:, :wide])

        def body(re, im, late, early, whole=whole, wide=wide):
            a_own, a_other, c_own, c_other = (load(spec, j, re, im, wide) for j in range(4))
            c_far = late(load(spec, 4, re, im, wide))
            h_own, h_all = ((x[re, whole], x[im, whole]) for x in (tap_spec, tap_all))
            h_other = load(near_spec, 0, re, im, wide)
            store(high, 0, re, im, times(a_own, h_own))
            store(high, 1, re, im, times(a_other, h_other))
            store(high, 2, re, im, plus(conj_times(h_own, c_own), conj_times(h_all, c_far)))
            store(high, 3, re, im, conj_times(h_other, c_other))
            store(high, 4, re, im, early(times(a_own, h_all)))
            store(high, 5, re, im, conj_times(a_own, plus(c_own, c_far)))
            store(high, 6, re, im, early(conj_times(a_own, c_far)))
            store(high, 7, re, im, conj_times(a_other, c_other))

        by_strips(length, wide, body)
        conv[:, : 5 * wide] = dot(inv_data, high[:, : 5 * wide]).astype(jnp.bfloat16)
        grads[:, : 3 * wide] = dot(chosen(inv, 0), high[:, 5 * wide : 8 * wide])
        for r in range(half):
            rows = pl.ds(pl.multiple_of(after(place, r, half) * block, block), block)
            for j in range(4):
                pair_outs[r][j, :, cols] = conv[rows, j * wide : (j + 1) * wide]
            cross_outs[r][:, cols] = conv[rows, 4 * wide : 5 * wide]
        for j in range(3):
            split_lags(grads, j, keep, whole, send, j * length // 2, replicas, core)


def tiles(width, tile):
    return [slice(i, min(i + tile, width)) for i in range(0, width, tile)]


def spectral(kernel, tile, info, operands, shapes, scratch, cost, aliases={}):
    tile = min(tile, shapes[0][0][-1])
    vmem = pl.BlockSpec(memory_space=pltpu.VMEM)
    return pl.pallas_call(
        functools.partial(kernel, tile),
        in_specs=[pl.BlockSpec(memory_space=pltpu.SMEM)] + [vmem] * len(operands),
        out_specs=[vmem] * len(shapes),
        scratch_shapes=[pltpu.VMEM((r, n * tile), t) for r, n, t in scratch],
        out_shape=[jax.ShapeDtypeStruct(s, t) for s, t in shapes],
        compiler_params=pltpu.CompilerParams(vmem_limit_bytes=VMEM),
        input_output_aliases=aliases,
        cost_estimate=cost,
    )(info, *operands)


def finish_kernel(half, start, info, *refs):
    received = refs[: 2 * half]
    grad, value, key = refs[2 * half : 2 * half + 3]
    *outs, made, sems = refs[-5:]
    lower = info[0] == 0
    width = made.shape[3]
    group = grad.shape[1] // (2 * half)
    copies = []
    for s in range(2 * half):
        r, other = s // 2, s % 2
        pair, cross = received[r], received[half + r]
        col = group_of(info, before(info[1], r, half), other, half) * group + start
        cols = pl.ds(pl.multiple_of(col, 128), width)
        first = pair[other].astype(jnp.float32)
        second = pair[2 + other].astype(jnp.float32)
        if other:
            second += cross[...].astype(jnp.float32)
            second = second.astype(jnp.bfloat16).astype(jnp.float32)
        conv = jnp.where(lower, first, second)
        back = jnp.where(lower, second, first)
        for i, (x, row) in enumerate(((conv, grad), (back, value), (back, key))):
            made[i, s] = (x * row[:, cols].astype(jnp.float32)).astype(jnp.bfloat16)
            copies.append(pltpu.make_async_copy(made.at[i, s], outs[i].at[:, cols], sems.at[i, s]))
            copies[-1].start()
    for copy in copies:
        copy.wait()


def finish(info, half, start, pairs, crosses, grad, value, key, earlier):
    tokens, width = crosses[0].shape
    vmem, anywhere = pl.BlockSpec(memory_space=pltpu.VMEM), pl.BlockSpec(memory_space=pl.ANY)
    return pl.pallas_call(
        functools.partial(finish_kernel, half, start),
        in_specs=[pl.BlockSpec(memory_space=pltpu.SMEM)]
        + [vmem] * (2 * half + 3)
        + [anywhere] * len(earlier),
        out_specs=[anywhere] * 3,
        out_shape=[jax.ShapeDtypeStruct(grad.shape, jnp.bfloat16)] * 3,
        scratch_shapes=[
            pltpu.VMEM((3, 2 * half, tokens, width), jnp.bfloat16),
            pltpu.SemaphoreType.DMA((3, 2 * half)),
        ],
        input_output_aliases={2 * half + 4 + i: i for i in range(len(earlier))},
        compiler_params=pltpu.CompilerParams(vmem_limit_bytes=VMEM),
        cost_estimate=large if earlier else tiny,
    )(info, *pairs, *crosses, grad, value, key, *earlier)


def sum_kernel(keep, *refs):
    *sends, own, other = refs
    rows = own.shape[0]
    start = 0
    for send in sends:
        cols = slice(start, start + send.shape[1])
        start = cols.stop
        own[:, cols] = keep[:rows, cols] + send[:rows, :].astype(jnp.float32)
        total = keep[rows:, cols] + send[rows:, :].astype(jnp.float32)
        other[:, cols] = total.astype(other.dtype)


def last_kernel(bit, info, own, over, go, stay):
    upper = info[2] & bit != 0
    first, second = own[0] + over[...].astype(jnp.float32), own[1]
    go[...] = jnp.where(upper, first, second).astype(go.dtype)
    stay[...] = jnp.where(upper, second, first)


def halve(x, bit, replicas, wire):
    upper = lax.axis_index("dp") & bit != 0
    x = x.reshape(-1, 2, *x.shape[1:])
    go = jnp.where(upper, x[:, 0], x[:, 1]).astype(wire)
    stay = jnp.where(upper, x[:, 1], x[:, 0])
    return stay + lax.ppermute(go, "dp", flip(replicas, bit)).astype(jnp.float32)


def sum_lags(keep, sends, length, replicas):
    sends = [lax.ppermute(x, "dp", flip(replicas, 1)) for x in sends]
    vmem = pl.BlockSpec(memory_space=pltpu.VMEM)
    width = keep.shape[1]
    own, other = pl.pallas_call(
        sum_kernel,
        in_specs=[vmem] * (1 + len(sends)),
        out_specs=[vmem, vmem],
        out_shape=[
            jax.ShapeDtypeStruct((length, width), jnp.float32),
            jax.ShapeDtypeStruct(
                (length // 2, width), jnp.bfloat16 if replicas == 4 else jnp.float32
            ),
        ],
        compiler_params=pltpu.CompilerParams(vmem_limit_bytes=VMEM),
        cost_estimate=tiny,
    )(keep, *sends)
    lags = 2 * length // replicas
    own, other = own.reshape(-1, lags, width), other.reshape(-1, lags, width)
    bit = 2
    while bit < replicas // 2:
        own, other = (halve(x, bit, replicas, jnp.float32) for x in (own, other))
        bit *= 2
    return own, other[0].astype(jnp.bfloat16)


def local(replicas, half, query, key, value, grad, taps):
    place = lax.axis_index("seq")
    info = jnp.stack([place // half, place % half, lax.axis_index("dp")]).astype(jnp.int32)
    length, width = taps.shape[0] // 2, taps.shape[1]
    block = query.shape[0]
    f32, bf16 = jnp.float32, jnp.bfloat16
    forward, inverse = (jnp.asarray(t) for t in tables(length))

    def pass_on(pairs):
        return [lax.ppermute(x, "seq", hop(half, 0, r)) if r else x for r, x in enumerate(pairs)]

    def pass_over(crosses):
        return [lax.ppermute(x, "seq", hop(half, 1, r)) for r, x in enumerate(crosses)]

    cut = width * 5 // 8 // 128 * 128
    spans = [slice(0, cut), slice(cut, width)] if cut else [slice(0, width)]
    pairs, crosses, near = gate(info, half, spans, (query, key, value, grad), taps)
    near = lax.ppermute(near, "seq", hop(half, 1, 0))
    tap_specs = spectral(
        taps_kernel,
        256,
        info,
        [taps, forward],
        [((2 * length, width), f32)] * 2,
        [(length, 2, bf16), (length, 2, bf16)],
        tiny,
    )
    pairs, crosses[0] = [pass_on(x) for x in pairs], pass_over(crosses[0])
    for c in range(1, len(spans)):
        crosses[c], (pairs[0], crosses[0], near, tap_specs) = lax.optimization_barrier(
            (crosses[c], (pairs[0], crosses[0], near, tap_specs))
        )
        crosses[c] = pass_over(crosses[c])
    near = (near, lax.ppermute(near, "dp", flip(replicas, 1)))
    results, cross_results, keep, sends = [], [], [], []
    for c, cols in enumerate(spans):
        wide = cols.stop - cols.start
        outs = spectral(
            functools.partial(conv_kernel, half, replicas, cols.start),
            256,
            info,
            [*pairs[c], *crosses[c], *tap_specs, *near, forward, inverse, *keep],
            [((4, block, wide), bf16)] * half
            + [((block, wide), bf16)] * half
            + [((3 * length // 2, width), f32)]
            + [((3 * length // 2, t.stop - t.start), bf16) for t in tiles(wide, 256)],
            [
                (length, 5, bf16),
                (length, 1, bf16),
                (2 * length, 5, f32),
                (2 * length, 1, f32),
                (2 * length, 8, bf16),
                (length, 5, bf16),
                (length, 3, f32),
            ],
            large,
            {2 * half + 7: 2 * half} if c else {},
        )
        keep, *more = outs[2 * half :]
        keep, sends = [keep], sends + more
        cross = list(outs[half : 2 * half])
        if c:
            sends, cross_results[-1] = lax.optimization_barrier((sends, cross_results[-1]))
            cross[-1], results[-1] = lax.optimization_barrier((cross[-1], results[-1]))
        results.append(pass_on(outs[:half]))
        cross_results.append(pass_over(cross))
    own, other = sum_lags(*keep, sends, length, replicas)
    other = lax.ppermute(other, "seq", hop(half, 1, 0))
    outs = []
    for c, cols in enumerate(spans):
        outs = finish(info, half, cols.start, results[c], cross_results[c], grad, value, key, outs)
    vmem = pl.BlockSpec(memory_space=pltpu.VMEM)
    bit = replicas // 2
    go, stay = pl.pallas_call(
        functools.partial(last_kernel, bit),
        in_specs=[pl.BlockSpec(memory_space=pltpu.SMEM), vmem, vmem],
        out_specs=[vmem, vmem],
        out_shape=[jax.ShapeDtypeStruct(other.shape, t) for t in (bf16, f32)],
        compiler_params=pltpu.CompilerParams(vmem_limit_bytes=VMEM),
        cost_estimate=tiny,
    )(info, own, other)
    grad_filter = stay + lax.ppermute(go, "dp", flip(replicas, bit)).astype(f32)
    return *outs, grad_filter


def solution(mesh):
    rows = P(("dp", "seq"), "chan")
    return jax.shard_map(
        functools.partial(local, mesh.shape["dp"], mesh.shape["seq"] // 2),
        mesh=mesh,
        in_specs=(rows, rows, rows, rows, P(None, ("chan", "seq"))),
        out_specs=(rows, rows, rows, P("dp", ("chan", "seq"))),
        check_vma=False,
    )
```

```python
import functools

import jax
import jax.numpy as jnp
import ml_dtypes
import numpy as np
from jax import lax
from jax.experimental import pallas as pl
from jax.experimental.pallas import tpu as pltpu
from jax.sharding import PartitionSpec as P


def split_bf16(x):
    high = x.astype(ml_dtypes.bfloat16)
    return np.concatenate([high, (x - high.astype(np.float64)).astype(ml_dtypes.bfloat16)])


@functools.cache
def tables(half_len):
    freq = 2 * np.arange(half_len)[:, None] + 1
    angles = np.pi * (freq * np.arange(half_len)[None, :] % (4 * half_len)) / (2 * half_len)
    forward = np.concatenate([np.cos(angles), -np.sin(angles)], axis=0)
    both = [forward, forward[:, ::-1]]
    return (
        np.concatenate([split_bf16(m) for m in both]),
        np.concatenate([(m.T / half_len).astype(ml_dtypes.bfloat16) for m in both]),
    )


VMEM = 12 << 20
tiny = pl.CostEstimate(flops=0, bytes_accessed=1, transcendentals=0)
large = pl.CostEstimate(flops=1 << 35, bytes_accessed=1, transcendentals=0)


def hop(half, across, steps):
    return [
        (h * half + p, (h ^ across) * half + (p + steps) % half)
        for h in (0, 1)
        for p in range(half)
    ]


def flip(size, bit):
    return [(d, d ^ bit) for d in range(size)]


def after(place, steps, half):
    return lax.rem(place + steps, half)


def before(place, steps, half):
    return lax.rem(place + half - steps, half)


def position(half):
    device = lax.axis_index("seq")
    return device // half, device % half, lax.axis_index("dp")


def group_of(info, place, other, half):
    side = 1 - info[0] if other else info[0]
    return side * half + place


def gate_kernel(half, start, *refs):
    outputs, held, sems = refs[5 - bool(start) : 5 - bool(start) + 2 * half], refs[-2], refs[-1]
    info = position(half)
    lower = info[0] == 0
    block, width = held.shape[2:]
    group = refs[0].shape[1] // (2 * half)
    copies = []
    for s in range(2 * half):
        col = group_of(info, after(info[1], s // 2, half), s % 2, half) * group + start
        cols = pl.ds(pl.multiple_of(col, 128), width)
        for i, row in enumerate(refs[:4]):
            copies.append(pltpu.make_async_copy(row.at[:, cols], held.at[i, s], sems.at[i, s]))
            copies[-1].start()
    if not start:
        taps, held_taps, taps_sem = refs[4], refs[-4], refs[-3]
        piece = held_taps.shape[0]
        mine = pl.ds(pl.multiple_of(info[2] % 2 * piece, piece), piece)
        taps_copy = pltpu.make_async_copy(taps.at[mine, :], held_taps, taps_sem)
        taps_copy.start()
    for s in range(2 * half):
        for copy in copies[4 * s : 4 * s + 4]:
            copy.wait()
        r, t = s // 2, s % 2
        pair, cross = outputs[r], outputs[half + r]
        query, key, value, grad = (held[i, s].astype(jnp.float32) for i in range(4))
        mixed, scaled = key * value, grad * query
        first = jnp.where(lower, mixed, scaled).astype(jnp.bfloat16)
        pair[t] = first
        pair[2 + t] = jnp.where(lower, scaled, mixed).astype(jnp.bfloat16)
        if t and (start or r):
            cross[...] = first
        elif t:
            for j in range(width // 128):
                cross[j * block : (j + 1) * block, :] = first[:, j * 128 : (j + 1) * 128]
    if not start:
        taps_copy.wait()
        base = width // 128 * block
        for j in range(group // 128):
            part = held_taps[:, j * 128 : (j + 1) * 128].astype(jnp.bfloat16)
            outputs[half][base + j * piece : base + (j + 1) * piece, :] = part


def gate(half, cols, rows, taps):
    tokens, channels = rows[0].shape
    group = channels // (2 * half)
    width, piece = cols.stop - cols.start, taps.shape[0] // 4
    shapes = [(4, tokens, width)] * half + [(tokens, width)] * half
    scratch = [
        pltpu.VMEM((4, 2 * half, tokens, width), jnp.bfloat16),
        pltpu.SemaphoreType.DMA((4, 2 * half)),
    ]
    operands = list(rows)
    if not cols.start:
        shapes[half] = ((width * tokens + group * piece) // 128, 128)
        scratch = [pltpu.VMEM((piece, group), jnp.float32), pltpu.SemaphoreType.DMA] + scratch
        operands.append(taps)
    outs = pl.pallas_call(
        functools.partial(gate_kernel, half, cols.start),
        in_specs=[pl.BlockSpec(memory_space=pl.ANY)] * len(operands),
        out_specs=[pl.BlockSpec(memory_space=pltpu.VMEM)] * len(shapes),
        out_shape=[jax.ShapeDtypeStruct(s, jnp.bfloat16) for s in shapes],
        scratch_shapes=scratch,
        compiler_params=pltpu.CompilerParams(vmem_limit_bytes=56 << 20),
        cost_estimate=tiny,
    )(*operands)
    return outs[:half], outs[half:]


def high_low(x):
    high = x.astype(jnp.bfloat16)
    return high, (x - high.astype(jnp.float32)).astype(jnp.bfloat16)


def dot(a, b):
    return jnp.dot(a, b, preferred_element_type=jnp.float32)


def times(a, b):
    return a[0] * b[0] - a[1] * b[1], a[0] * b[1] + a[1] * b[0]


def conj_times(a, b):
    return a[0] * b[0] + a[1] * b[1], a[0] * b[1] - a[1] * b[0]


def plus(a, b):
    return a[0] + b[0], a[1] + b[1]


def load(ref, j, re, im, width):
    cols = slice(j * width, (j + 1) * width)
    return ref[re, cols], ref[im, cols]


def store(ref, j, re, im, x):
    width = x[0].shape[1]
    cols = slice(j * width, (j + 1) * width)
    ref[re, cols] = x[0].astype(ref.dtype)
    ref[im, cols] = x[1].astype(ref.dtype)


def by_strips(length, width, body):
    strip = 16
    odd = lax.broadcasted_iota(jnp.int32, (strip, width), 0) % 2
    sign = (1 - 2 * odd).astype(jnp.float32)

    def late(x):
        return sign * x[1], -sign * x[0]

    def early(x):
        return -sign * x[1], sign * x[0]

    def step(i, carry):
        re = pl.ds(pl.multiple_of(i * strip, strip), strip)
        im = pl.ds(pl.multiple_of(length + i * strip, strip), strip)
        body(re, im, late, early)
        return carry

    lax.fori_loop(0, length // strip, step, 0, unroll=4)


def chosen(table, side):
    rows = table.shape[0] // 2
    return table[pl.ds(pl.multiple_of(side * rows, rows), rows), :]


def transform(matrix, x):
    rows = matrix.shape[0] // 2
    return dot(matrix[:rows], x) + dot(matrix[rows:], x)


def place_rows(target, j, sources, cols, place, half):
    block, width = sources[0].shape[0], cols.stop - cols.start
    for r, source in enumerate(sources):
        rows = pl.ds(pl.multiple_of(before(place, r, half) * block, block), block)
        target[rows, j * width : (j + 1) * width] = source[:, cols]


def split_lags(grads, j, keep, cols, send, row, replicas, core):
    lags, width = 2 * grads.shape[0] // replicas, cols.stop - cols.start
    for ref, cols, mine in ((keep, cols, core), (send, slice(0, width), 1 - core)):
        for i in range(replicas // 4):
            rows = pl.ds(pl.multiple_of((2 * i + mine) * lags, lags), lags)
            part = grads[rows, j * width : (j + 1) * width]
            ref[row + i * lags : row + (i + 1) * lags, cols] = part.astype(ref.dtype)


def taps_kernel(tile, taps, fwd, near_spec, all_spec, high, low):
    length = taps.shape[0] // 2
    matrix = chosen(fwd, 0)
    for cols in tiles(taps.shape[1], tile):
        for j in (0, 1):
            part = slice(j * tile, (j + 1) * tile)
            high[:, part], low[:, part] = high_low(taps[j * length : (j + 1) * length, cols])
        spec = transform(matrix, high[...]) + dot(matrix[: 2 * length], low[...])
        near_spec[:, cols] = spec[:, :tile]
        all_spec[:, cols] = spec[:, tile:]

        def body(re, im, late, early, cols=cols):
            far = late((all_spec[re, cols], all_spec[im, cols]))
            all_spec[re, cols] = near_spec[re, cols] + far[0]
            all_spec[im, cols] = near_spec[im, cols] + far[1]

        by_strips(length, tile, body)


def conv_kernel(half, replicas, start, tile, *refs):
    pairs, crosses, refs = refs[:half], refs[half : 2 * half], refs[2 * half :]
    tap_spec, tap_all, first_cross, near, fwd, inv = refs[:6]
    refs = refs[7 if start else 6 :]
    pair_outs, cross_outs, keep = refs[:half], refs[half : 2 * half], refs[2 * half]
    *sends, data, near_all, spec, near_spec, high, conv, grads = refs[2 * half + 1 :]
    side, place, replica = position(half)
    core = replica % 2
    _, block, width = pairs[0].shape
    length = half * block
    piece = length // 2
    fwd_data, inv_data = chosen(fwd, side), chosen(inv, side)
    for cols, send in zip(tiles(width, tile), sends, strict=True):
        wide = cols.stop - cols.start
        whole = slice(start + cols.start, start + cols.stop)
        for j in range(4):
            place_rows(data, j, [pair.at[j] for pair in pairs], cols, place, half)
        if start:
            place_rows(data, 4, crosses, cols, place, half)
        for j in range(0 if start else wide // 128):
            k = cols.start // 128 + j
            parts = [crosses[0].at[k * block : (k + 1) * block]]
            parts += [cross.at[:, k * 128 : (k + 1) * 128] for cross in crosses[1:]]
            place_rows(data, 4 * wide // 128 + j, parts, slice(0, 128), place, half)
        for mine, source in ((core, first_cross), (1 - core, near)):
            rows = pl.ds(pl.multiple_of(mine * piece, piece), piece)
            base = source.shape[0] - near.shape[0]
            for j in range(wide // 128):
                k = base + (whole.start // 128 + j) * piece
                near_all[rows, j * 128 : (j + 1) * 128] = source[k : k + piece, :]
        spec[:, : 5 * wide] = transform(fwd_data, data[:, : 5 * wide])
        near_spec[:, :wide] = transform(chosen(fwd, 0), near_all[:, :wide])

        def body(re, im, late, early, whole=whole, wide=wide):
            a_own, a_other, c_own, c_other = (load(spec, j, re, im, wide) for j in range(4))
            c_far = late(load(spec, 4, re, im, wide))
            h_own, h_all = ((x[re, whole], x[im, whole]) for x in (tap_spec, tap_all))
            h_other = load(near_spec, 0, re, im, wide)
            store(high, 0, re, im, times(a_own, h_own))
            store(high, 1, re, im, times(a_other, h_other))
            store(high, 2, re, im, plus(conj_times(h_own, c_own), conj_times(h_all, c_far)))
            store(high, 3, re, im, conj_times(h_other, c_other))
            store(high, 4, re, im, early(times(a_own, h_all)))
            store(high, 5, re, im, conj_times(a_own, plus(c_own, c_far)))
            store(high, 6, re, im, early(conj_times(a_own, c_far)))
            store(high, 7, re, im, conj_times(a_other, c_other))

        by_strips(length, wide, body)
        conv[:, : 5 * wide] = dot(inv_data, high[:, : 5 * wide]).astype(jnp.bfloat16)
        grads[:, : 3 * wide] = dot(chosen(inv, 0), high[:, 5 * wide : 8 * wide])
        for r in range(half):
            rows = pl.ds(pl.multiple_of(after(place, r, half) * block, block), block)
            for j in range(4):
                pair_outs[r][j, :, cols] = conv[rows, j * wide : (j + 1) * wide]
            cross_outs[r][:, cols] = conv[rows, 4 * wide : 5 * wide]
        for j in range(3):
            split_lags(grads, j, keep, whole, send, j * length // 2, replicas, core)


def tiles(width, tile):
    return [slice(i, min(i + tile, width)) for i in range(0, width, tile)]


def spectral(kernel, tile, operands, shapes, scratch, cost, aliases={}):
    tile = min(tile, shapes[0][0][-1])
    vmem = pl.BlockSpec(memory_space=pltpu.VMEM)
    return pl.pallas_call(
        functools.partial(kernel, tile),
        in_specs=[vmem] * len(operands),
        out_specs=[vmem] * len(shapes),
        scratch_shapes=[pltpu.VMEM((r, n * tile), t) for r, n, t in scratch],
        out_shape=[jax.ShapeDtypeStruct(s, t) for s, t in shapes],
        compiler_params=pltpu.CompilerParams(vmem_limit_bytes=VMEM),
        input_output_aliases=aliases,
        cost_estimate=cost,
    )(*operands)


def finish_kernel(half, start, *refs):
    received = refs[: 2 * half]
    grad, value, key = refs[2 * half : 2 * half + 3]
    *outs, made, sems = refs[-5:]
    info = position(half)
    lower = info[0] == 0
    width = made.shape[3]
    group = grad.shape[1] // (2 * half)
    copies = []
    for s in range(2 * half):
        r, other = s // 2, s % 2
        pair, cross = received[r], received[half + r]
        col = group_of(info, before(info[1], r, half), other, half) * group + start
        cols = pl.ds(pl.multiple_of(col, 128), width)
        first = pair[other].astype(jnp.float32)
        second = pair[2 + other].astype(jnp.float32)
        if other:
            second += cross[...].astype(jnp.float32)
            second = second.astype(jnp.bfloat16).astype(jnp.float32)
        conv = jnp.where(lower, first, second)
        back = jnp.where(lower, second, first)
        for i, (x, row) in enumerate(((conv, grad), (back, value), (back, key))):
            made[i, s] = (x * row[:, cols].astype(jnp.float32)).astype(jnp.bfloat16)
            copies.append(pltpu.make_async_copy(made.at[i, s], outs[i].at[:, cols], sems.at[i, s]))
            copies[-1].start()
    for copy in copies:
        copy.wait()


def finish(half, start, pairs, crosses, grad, value, key, earlier):
    tokens, width = crosses[0].shape
    vmem, anywhere = pl.BlockSpec(memory_space=pltpu.VMEM), pl.BlockSpec(memory_space=pl.ANY)
    return pl.pallas_call(
        functools.partial(finish_kernel, half, start),
        in_specs=[vmem] * (2 * half + 3) + [anywhere] * len(earlier),
        out_specs=[anywhere] * 3,
        out_shape=[jax.ShapeDtypeStruct(grad.shape, jnp.bfloat16)] * 3,
        scratch_shapes=[
            pltpu.VMEM((3, 2 * half, tokens, width), jnp.bfloat16),
            pltpu.SemaphoreType.DMA((3, 2 * half)),
        ],
        input_output_aliases={2 * half + 3 + i: i for i in range(len(earlier))},
        compiler_params=pltpu.CompilerParams(vmem_limit_bytes=VMEM),
        cost_estimate=large if earlier else tiny,
    )(*pairs, *crosses, grad, value, key, *earlier)


def sum_kernel(keep, *refs):
    *sends, own, other = refs
    rows = own.shape[0]
    start = 0
    for send in sends:
        cols = slice(start, start + send.shape[1])
        start = cols.stop
        total = keep[:, cols] + send[...].astype(jnp.float32)
        own[:, cols] = total[:rows]
        other[:, cols] = total[rows:].astype(other.dtype)


def last_kernel(bit, own, over, stay, go):
    upper = lax.axis_index("dp") & bit != 0
    lags = over.shape[0]
    first, second = own[:lags] + over[...].astype(jnp.float32), own[lags:]
    stay[...] = jnp.where(upper, second, first)
    go[...] = jnp.where(upper, first, second).astype(go.dtype)


def add_kernel(stay, arrived, out):
    out[...] = stay[...] + arrived[...].astype(jnp.float32)


def halve(x, bit):
    upper = lax.axis_index("dp") & bit != 0
    x = x.reshape(-1, 2, *x.shape[1:])
    return jnp.where(upper, x[:, 1], x[:, 0]), jnp.where(upper, x[:, 0], x[:, 1])


def in_vmem(kernel, operands, shapes):
    vmem = pl.BlockSpec(memory_space=pltpu.VMEM)
    return pl.pallas_call(
        kernel,
        in_specs=[vmem] * len(operands),
        out_specs=[vmem] * len(shapes),
        out_shape=[jax.ShapeDtypeStruct(s, t) for s, t in shapes],
        compiler_params=pltpu.CompilerParams(vmem_limit_bytes=VMEM),
        cost_estimate=tiny,
    )(*operands)


def sum_filter(keep, sends, length, half, replicas):
    f32, bf16 = jnp.float32, jnp.bfloat16
    lags, width = 2 * length // replicas, keep.shape[1]
    sends = [lax.ppermute(x, "dp", flip(replicas, 1)) for x in sends]
    own, other = in_vmem(
        sum_kernel,
        [keep, *sends],
        [((length, width), f32), ((length // 2, width), bf16 if replicas == 4 else f32)],
    )
    bit = 2
    while bit < replicas // 2:
        own, other = (
            stay + lax.ppermute(go, "dp", flip(replicas, bit))
            for stay, go in (halve(x.reshape(-1, lags, width), bit) for x in (own, other))
        )
        bit *= 2
    own, other = own.reshape(-1, width), other.reshape(-1, width).astype(bf16)
    over = lax.ppermute(other, "seq", hop(half, 1, 0))
    stay, go = in_vmem(
        functools.partial(last_kernel, bit),
        [own, over],
        [((lags, width), f32), ((lags, width), bf16)],
    )
    arrived = lax.ppermute(go, "dp", flip(replicas, bit))
    return in_vmem(add_kernel, [stay, arrived], [(stay.shape, f32)])[0]


def local(replicas, half, query, key, value, grad, taps):
    length, width = taps.shape[0] // 2, taps.shape[1]
    block = query.shape[0]
    f32, bf16 = jnp.float32, jnp.bfloat16
    forward, inverse = (jnp.asarray(t) for t in tables(length))
    cut = width * 5 // 8 // 128 * 128
    cut = cut or width
    spans = [slice(0, cut), slice(cut, width)] if cut < width else [slice(0, width)]

    def pass_on(pairs):
        return [lax.ppermute(x, "seq", hop(half, 0, r)) if r else x for r, x in enumerate(pairs)]

    def pass_over(crosses):
        return [lax.ppermute(x, "seq", hop(half, 1, r)) for r, x in enumerate(crosses)]

    def tie(*parts):
        return lax.optimization_barrier(parts)

    gated = [gate(half, cols, (query, key, value, grad), taps) for cols in spans]
    pairs, crosses = [list(x) for x in zip(*gated, strict=True)]
    tap_specs = spectral(
        taps_kernel,
        256,
        [taps, forward],
        [((2 * length, width), f32)] * 2,
        [(length, 2, bf16), (length, 2, bf16)],
        tiny,
    )
    pairs[0], crosses[0] = pass_on(pairs[0]), pass_over(crosses[0])
    for c in range(1, len(spans)):
        pairs[c], crosses[c], pairs[0], crosses[0], tap_specs = tie(
            pairs[c], crosses[c], pairs[0], crosses[0], tap_specs
        )
        pairs[c], crosses[c] = pass_on(pairs[c]), pass_over(crosses[c])
    near = lax.ppermute(crosses[0][0][cut * block // 128 :], "dp", flip(replicas, 1))
    results, cross_results, keep, sends = [], [], [], []
    for c, cols in enumerate(spans):
        wide = cols.stop - cols.start
        outs = spectral(
            functools.partial(conv_kernel, half, replicas, cols.start),
            256,
            [*pairs[c], *crosses[c], *tap_specs, crosses[0][0], near, forward, inverse, *keep],
            [((4, block, wide), bf16)] * half
            + [((block, wide), bf16)] * half
            + [((3 * length // 2, width), f32)]
            + [((3 * length // 2, t.stop - t.start), bf16) for t in tiles(wide, 256)],
            [
                (length, 5, bf16),
                (length, 1, bf16),
                (2 * length, 5, f32),
                (2 * length, 1, f32),
                (2 * length, 8, bf16),
                (length, 5, bf16),
                (length, 3, f32),
            ],
            large,
            {2 * half + 6: 2 * half} if c else {},
        )
        keep, *more = outs[2 * half :]
        keep, sends = [keep], sends + more
        cross = list(outs[half : 2 * half])
        if c:
            sends, cross_results[-1] = tie(sends, cross_results[-1])
        results.append(pass_on(outs[:half]))
        cross_results.append(pass_over(cross))
    grad_filter = sum_filter(*keep, sends, length, half, replicas)
    outs = []
    for c, cols in enumerate(spans):
        outs = finish(half, cols.start, results[c], cross_results[c], grad, value, key, outs)
    return *outs, grad_filter


def solution(mesh):
    rows = P(("dp", "seq"), "chan")
    return jax.shard_map(
        functools.partial(local, mesh.shape["dp"], mesh.shape["seq"] // 2),
        mesh=mesh,
        in_specs=(rows, rows, rows, rows, P(None, ("chan", "seq"))),
        out_specs=(rows, rows, rows, P("dp", ("chan", "seq"))),
        check_vma=False,
    )
```

```python
import functools

import jax
import jax.numpy as jnp
import ml_dtypes
import numpy as np
from jax import lax
from jax.experimental import pallas as pl
from jax.experimental.pallas import tpu as pltpu
from jax.sharding import PartitionSpec as P


def split_bf16(x):
    high = x.astype(ml_dtypes.bfloat16)
    return np.concatenate([high, (x - high.astype(np.float64)).astype(ml_dtypes.bfloat16)])


@functools.cache
def tables(half_len):
    freq = 2 * np.arange(half_len)[:, None] + 1
    angles = np.pi * (freq * np.arange(half_len)[None, :] % (4 * half_len)) / (2 * half_len)
    forward = np.concatenate([np.cos(angles), -np.sin(angles)], axis=0)
    both = [forward, forward[:, ::-1]]
    return (
        np.concatenate([split_bf16(m) for m in both]),
        np.concatenate([(m.T / half_len).astype(ml_dtypes.bfloat16) for m in both]),
    )


VMEM = 12 << 20
tiny = pl.CostEstimate(flops=0, bytes_accessed=1, transcendentals=0)
large = pl.CostEstimate(flops=1 << 35, bytes_accessed=1, transcendentals=0)


def hop(half, across, steps):
    return [
        (h * half + p, (h ^ across) * half + (p + steps) % half)
        for h in (0, 1)
        for p in range(half)
    ]


def flip(size, bit):
    return [(d, d ^ bit) for d in range(size)]


def after(place, steps, half):
    return lax.rem(place + steps, half)


def before(place, steps, half):
    return lax.rem(place + half - steps, half)


def position(half):
    device = lax.axis_index("seq")
    return device // half, device % half, lax.axis_index("dp")


def group_of(info, place, other, half):
    side = 1 - info[0] if other else info[0]
    return side * half + place


def gate_kernel(half, start, *refs):
    outputs, held, sems = refs[5 - bool(start) : 5 - bool(start) + 2 * half], refs[-2], refs[-1]
    info = position(half)
    lower = info[0] == 0
    block, width = held.shape[2:]
    group = refs[0].shape[1] // (2 * half)
    copies = []
    for s in range(2 * half):
        col = group_of(info, after(info[1], s // 2, half), s % 2, half) * group + start
        cols = pl.ds(pl.multiple_of(col, 128), width)
        for i, row in enumerate(refs[:4]):
            copies.append(pltpu.make_async_copy(row.at[:, cols], held.at[i, s], sems.at[i, s]))
            copies[-1].start()
    if not start:
        taps, held_taps, taps_sem = refs[4], refs[-4], refs[-3]
        piece = held_taps.shape[0]
        mine = pl.ds(pl.multiple_of(info[2] % 2 * piece, piece), piece)
        taps_copy = pltpu.make_async_copy(taps.at[mine, :], held_taps, taps_sem)
        taps_copy.start()
    for s in range(2 * half):
        for copy in copies[4 * s : 4 * s + 4]:
            copy.wait()
        r, t = s // 2, s % 2
        pair, cross = outputs[r], outputs[half + r]
        query, key, value, grad = (held[i, s].astype(jnp.float32) for i in range(4))
        mixed, scaled = key * value, grad * query
        first = jnp.where(lower, mixed, scaled).astype(jnp.bfloat16)
        pair[t] = first
        pair[2 + t] = jnp.where(lower, scaled, mixed).astype(jnp.bfloat16)
        if t and (start or r):
            cross[...] = first
        elif t:
            for j in range(width // 128):
                cross[j * block : (j + 1) * block, :] = first[:, j * 128 : (j + 1) * 128]
    if not start:
        taps_copy.wait()
        base = width // 128 * block
        for j in range(group // 128):
            part = held_taps[:, j * 128 : (j + 1) * 128].astype(jnp.bfloat16)
            outputs[half][base + j * piece : base + (j + 1) * piece, :] = part


def gate(half, cols, rows, taps):
    tokens, channels = rows[0].shape
    group = channels // (2 * half)
    width, piece = cols.stop - cols.start, taps.shape[0] // 4
    shapes = [(4, tokens, width)] * half + [(tokens, width)] * half
    scratch = [
        pltpu.VMEM((4, 2 * half, tokens, width), jnp.bfloat16),
        pltpu.SemaphoreType.DMA((4, 2 * half)),
    ]
    operands = list(rows)
    if not cols.start:
        shapes[half] = ((width * tokens + group * piece) // 128, 128)
        scratch = [pltpu.VMEM((piece, group), jnp.float32), pltpu.SemaphoreType.DMA] + scratch
        operands.append(taps)
    outs = pl.pallas_call(
        functools.partial(gate_kernel, half, cols.start),
        in_specs=[pl.BlockSpec(memory_space=pl.ANY)] * len(operands),
        out_specs=[pl.BlockSpec(memory_space=pltpu.VMEM)] * len(shapes),
        out_shape=[jax.ShapeDtypeStruct(s, jnp.bfloat16) for s in shapes],
        scratch_shapes=scratch,
        compiler_params=pltpu.CompilerParams(vmem_limit_bytes=56 << 20),
        cost_estimate=tiny,
    )(*operands)
    return outs[:half], outs[half:]


def high_low(x):
    high = x.astype(jnp.bfloat16)
    return high, (x - high.astype(jnp.float32)).astype(jnp.bfloat16)


def dot(a, b):
    return jnp.dot(a, b, preferred_element_type=jnp.float32)


def times(a, b):
    return a[0] * b[0] - a[1] * b[1], a[0] * b[1] + a[1] * b[0]


def conj_times(a, b):
    return a[0] * b[0] + a[1] * b[1], a[0] * b[1] - a[1] * b[0]


def plus(a, b):
    return a[0] + b[0], a[1] + b[1]


def load(ref, j, re, im, width):
    cols = slice(j * width, (j + 1) * width)
    return ref[re, cols], ref[im, cols]


def store(ref, j, re, im, x):
    width = x[0].shape[1]
    cols = slice(j * width, (j + 1) * width)
    ref[re, cols] = x[0].astype(ref.dtype)
    ref[im, cols] = x[1].astype(ref.dtype)


def by_strips(length, width, body):
    strip = 16
    odd = lax.broadcasted_iota(jnp.int32, (strip, width), 0) % 2
    sign = (1 - 2 * odd).astype(jnp.float32)

    def late(x):
        return sign * x[1], -sign * x[0]

    def early(x):
        return -sign * x[1], sign * x[0]

    def step(i, carry):
        re = pl.ds(pl.multiple_of(i * strip, strip), strip)
        im = pl.ds(pl.multiple_of(length + i * strip, strip), strip)
        body(re, im, late, early)
        return carry

    lax.fori_loop(0, length // strip, step, 0, unroll=4)


def chosen(table, side):
    rows = table.shape[0] // 2
    return table[pl.ds(pl.multiple_of(side * rows, rows), rows), :]


def transform(matrix, x):
    rows = matrix.shape[0] // 2
    return dot(matrix[:rows], x) + dot(matrix[rows:], x)


def place_rows(target, j, sources, cols, place, half):
    block, width = sources[0].shape[0], cols.stop - cols.start
    for r, source in enumerate(sources):
        rows = pl.ds(pl.multiple_of(before(place, r, half) * block, block), block)
        target[rows, j * width : (j + 1) * width] = source[:, cols]


def split_lags(grads, j, keep, cols, send, row, replicas, core):
    lags, width = 2 * grads.shape[0] // replicas, cols.stop - cols.start
    for ref, cols, mine in ((keep, cols, core), (send, slice(0, width), 1 - core)):
        for i in range(replicas // 4):
            rows = pl.ds(pl.multiple_of((2 * i + mine) * lags, lags), lags)
            part = grads[rows, j * width : (j + 1) * width]
            ref[row + i * lags : row + (i + 1) * lags, cols] = part.astype(ref.dtype)


def taps_kernel(tile, taps, fwd, near_spec, all_spec, high, low):
    length = taps.shape[0] // 2
    matrix = chosen(fwd, 0)
    for cols in tiles(taps.shape[1], tile):
        for j in (0, 1):
            part = slice(j * tile, (j + 1) * tile)
            high[:, part], low[:, part] = high_low(taps[j * length : (j + 1) * length, cols])
        spec = transform(matrix, high[...]) + dot(matrix[: 2 * length], low[...])
        near_spec[:, cols] = spec[:, :tile]
        all_spec[:, cols] = spec[:, tile:]

        def body(re, im, late, early, cols=cols):
            far = late((all_spec[re, cols], all_spec[im, cols]))
            all_spec[re, cols] = near_spec[re, cols] + far[0]
            all_spec[im, cols] = near_spec[im, cols] + far[1]

        by_strips(length, tile, body)


def conv_kernel(half, replicas, start, tile, *refs):
    pairs, crosses, refs = refs[:half], refs[half : 2 * half], refs[2 * half :]
    tap_spec, tap_all, first_cross, near, fwd, inv = refs[:6]
    refs = refs[7 if start else 6 :]
    pair_outs, cross_outs, keep = refs[:half], refs[half : 2 * half], refs[2 * half]
    *sends, data, near_all, spec, near_spec, high, conv, grads = refs[2 * half + 1 :]
    side, place, replica = position(half)
    core = replica % 2
    _, block, width = pairs[0].shape
    length = half * block
    piece = length // 2
    fwd_data, inv_data = chosen(fwd, side), chosen(inv, side)
    for cols, send in zip(tiles(width, tile), sends, strict=True):
        wide = cols.stop - cols.start
        whole = slice(start + cols.start, start + cols.stop)
        for j in range(4):
            place_rows(data, j, [pair.at[j] for pair in pairs], cols, place, half)
        if start:
            place_rows(data, 4, crosses, cols, place, half)
        for j in range(0 if start else wide // 128):
            k = cols.start // 128 + j
            parts = [crosses[0].at[k * block : (k + 1) * block]]
            parts += [cross.at[:, k * 128 : (k + 1) * 128] for cross in crosses[1:]]
            place_rows(data, 4 * wide // 128 + j, parts, slice(0, 128), place, half)
        for mine, source in ((core, first_cross), (1 - core, near)):
            rows = pl.ds(pl.multiple_of(mine * piece, piece), piece)
            base = source.shape[0] - near.shape[0]
            for j in range(wide // 128):
                k = base + (whole.start // 128 + j) * piece
                near_all[rows, j * 128 : (j + 1) * 128] = source[k : k + piece, :]
        spec[:, : 5 * wide] = transform(fwd_data, data[:, : 5 * wide])
        near_spec[:, :wide] = transform(chosen(fwd, 0), near_all[:, :wide])

        def body(re, im, late, early, whole=whole, wide=wide):
            a_own, a_other, c_own, c_other = (load(spec, j, re, im, wide) for j in range(4))
            c_far = late(load(spec, 4, re, im, wide))
            h_own, h_all = ((x[re, whole], x[im, whole]) for x in (tap_spec, tap_all))
            h_other = load(near_spec, 0, re, im, wide)
            store(high, 0, re, im, times(a_own, h_own))
            store(high, 1, re, im, times(a_other, h_other))
            store(high, 2, re, im, plus(conj_times(h_own, c_own), conj_times(h_all, c_far)))
            store(high, 3, re, im, conj_times(h_other, c_other))
            store(high, 4, re, im, early(times(a_own, h_all)))
            store(high, 5, re, im, conj_times(a_own, plus(c_own, c_far)))
            store(high, 6, re, im, early(conj_times(a_own, c_far)))
            store(high, 7, re, im, conj_times(a_other, c_other))

        by_strips(length, wide, body)
        conv[:, : 5 * wide] = dot(inv_data, high[:, : 5 * wide]).astype(jnp.bfloat16)
        grads[:, : 3 * wide] = dot(chosen(inv, 0), high[:, 5 * wide : 8 * wide])
        for r in range(half):
            rows = pl.ds(pl.multiple_of(after(place, r, half) * block, block), block)
            for j in range(4):
                pair_outs[r][j, :, cols] = conv[rows, j * wide : (j + 1) * wide]
            cross_outs[r][:, cols] = conv[rows, 4 * wide : 5 * wide]
        for j in range(3):
            split_lags(grads, j, keep, whole, send, j * length // 2, replicas, core)


def tiles(width, tile):
    return [slice(i, min(i + tile, width)) for i in range(0, width, tile)]


def spectral(kernel, tile, operands, shapes, scratch, cost, aliases={}):
    tile = min(tile, shapes[0][0][-1])
    vmem = pl.BlockSpec(memory_space=pltpu.VMEM)
    return pl.pallas_call(
        functools.partial(kernel, tile),
        in_specs=[vmem] * len(operands),
        out_specs=[vmem] * len(shapes),
        scratch_shapes=[pltpu.VMEM((r, n * tile), t) for r, n, t in scratch],
        out_shape=[jax.ShapeDtypeStruct(s, t) for s, t in shapes],
        compiler_params=pltpu.CompilerParams(vmem_limit_bytes=VMEM),
        input_output_aliases=aliases,
        cost_estimate=cost,
    )(*operands)


def finish_kernel(half, start, *refs):
    received = refs[: 2 * half]
    grad, value, key = refs[2 * half : 2 * half + 3]
    *outs, made, sems = refs[-5:]
    info = position(half)
    lower = info[0] == 0
    width = made.shape[3]
    group = grad.shape[1] // (2 * half)
    copies = []
    for s in range(2 * half):
        r, other = s // 2, s % 2
        pair, cross = received[r], received[half + r]
        col = group_of(info, before(info[1], r, half), other, half) * group + start
        cols = pl.ds(pl.multiple_of(col, 128), width)
        first = pair[other].astype(jnp.float32)
        second = pair[2 + other].astype(jnp.float32)
        if other:
            second += cross[...].astype(jnp.float32)
            second = second.astype(jnp.bfloat16).astype(jnp.float32)
        conv = jnp.where(lower, first, second)
        back = jnp.where(lower, second, first)
        for i, (x, row) in enumerate(((conv, grad), (back, value), (back, key))):
            made[i, s] = (x * row[:, cols].astype(jnp.float32)).astype(jnp.bfloat16)
            copies.append(pltpu.make_async_copy(made.at[i, s], outs[i].at[:, cols], sems.at[i, s]))
            copies[-1].start()
    for copy in copies:
        copy.wait()


def finish(half, start, pairs, crosses, grad, value, key, earlier):
    tokens, width = crosses[0].shape
    vmem, anywhere = pl.BlockSpec(memory_space=pltpu.VMEM), pl.BlockSpec(memory_space=pl.ANY)
    return pl.pallas_call(
        functools.partial(finish_kernel, half, start),
        in_specs=[vmem] * (2 * half + 3) + [anywhere] * len(earlier),
        out_specs=[anywhere] * 3,
        out_shape=[jax.ShapeDtypeStruct(grad.shape, jnp.bfloat16)] * 3,
        scratch_shapes=[
            pltpu.VMEM((3, 2 * half, tokens, width), jnp.bfloat16),
            pltpu.SemaphoreType.DMA((3, 2 * half)),
        ],
        input_output_aliases={2 * half + 3 + i: i for i in range(len(earlier))},
        compiler_params=pltpu.CompilerParams(vmem_limit_bytes=VMEM),
        cost_estimate=large if earlier else tiny,
    )(*pairs, *crosses, grad, value, key, *earlier)


def sum_kernel(replicas, keep, *refs):
    *sends, own, stay, go = refs
    rows = own.shape[0]
    upper = lax.axis_index("dp") & (replicas // 2) != 0
    start = 0
    for send in sends:
        cols = slice(start, start + send.shape[1])
        start = cols.stop
        total = keep[:, cols] + send[...].astype(jnp.float32)
        own[:, cols] = total[:rows]
        if replicas == 4:
            lags = (total.shape[0] - rows) // 2
            first, second = total[rows : rows + lags], total[rows + lags :]
            stay[:, cols] = jnp.where(upper, second, first)
            go[:, cols] = jnp.where(upper, first, second).astype(go.dtype)
        else:
            stay[:, cols] = total[rows:]
            go[:, cols] = jnp.zeros_like(go[:, cols])


def over_kernel(stay, arrived, out):
    out[...] = (stay[...] + arrived[...].astype(jnp.float32)).astype(out.dtype)


def add_kernel(stay, arrived, out):
    out[...] = stay[...] + arrived[...].astype(jnp.float32)


def last_kernel(bit, own, over, stay, go):
    upper = lax.axis_index("dp") & bit != 0
    lags, part = own.shape[0] // 2, over.shape[0]
    added = over[...].astype(jnp.float32)
    zeros = jnp.zeros_like(added)
    for i in (0, 1):
        rows = slice(i * part, (i + 1) * part)
        first = own[rows] + jnp.where(upper == bool(i), added, zeros)
        second = own[lags + i * part : lags + (i + 1) * part]
        stay[rows] = jnp.where(upper, second, first)
        go[rows] = jnp.where(upper, first, second).astype(go.dtype)


def halve(x, bit):
    upper = lax.axis_index("dp") & bit != 0
    x = x.reshape(-1, 2, *x.shape[1:])
    return jnp.where(upper, x[:, 1], x[:, 0]), jnp.where(upper, x[:, 0], x[:, 1])


def in_vmem(kernel, operands, shapes):
    vmem = pl.BlockSpec(memory_space=pltpu.VMEM)
    return pl.pallas_call(
        kernel,
        in_specs=[vmem] * len(operands),
        out_specs=[vmem] * len(shapes),
        out_shape=[jax.ShapeDtypeStruct(s, t) for s, t in shapes],
        compiler_params=pltpu.CompilerParams(vmem_limit_bytes=VMEM),
        cost_estimate=tiny,
    )(*operands)


def sum_filter(keep, sends, length, half, replicas):
    f32, bf16 = jnp.float32, jnp.bfloat16
    lags, width = 2 * length // replicas, keep.shape[1]
    sends = [lax.ppermute(x, "dp", flip(replicas, 1)) for x in sends]
    once = replicas == 4
    own, stay, go = in_vmem(
        functools.partial(sum_kernel, replicas),
        [keep, *sends],
        [
            ((length, width), f32),
            ((lags // 2 if once else length // 2, width), f32),
            ((lags // 2, width), bf16),
        ],
    )
    bit = 2
    if not once:
        own, other = own.reshape(-1, lags, width), stay.reshape(-1, lags, width)
        while bit < replicas // 2:
            own, other = (
                stay + lax.ppermute(go, "dp", flip(replicas, bit))
                for stay, go in (halve(x, bit) for x in (own, other))
            )
            bit *= 2
        stay, go = (x[0] for x in halve(other.reshape(2, lags // 2, width), bit))
        own, go = own.reshape(-1, width), go.astype(bf16)
    arrived = lax.ppermute(go, "dp", flip(replicas, bit))
    (other,) = in_vmem(over_kernel, [stay, arrived], [(stay.shape, bf16)])
    over = lax.ppermute(other, "seq", hop(half, 1, 0))
    stay, go = in_vmem(
        functools.partial(last_kernel, bit),
        [own, over],
        [((lags, width), f32), ((lags, width), bf16)],
    )
    arrived = lax.ppermute(go, "dp", flip(replicas, bit))
    return in_vmem(add_kernel, [stay, arrived], [(stay.shape, f32)])[0]


def local(replicas, half, query, key, value, grad, taps):
    length, width = taps.shape[0] // 2, taps.shape[1]
    block = query.shape[0]
    f32, bf16 = jnp.float32, jnp.bfloat16
    forward, inverse = (jnp.asarray(t) for t in tables(length))
    cut = width * 5 // 8 // 128 * 128
    cut = cut or width
    spans = [slice(0, cut), slice(cut, width)] if cut < width else [slice(0, width)]

    def pass_on(pairs):
        return [lax.ppermute(x, "seq", hop(half, 0, r)) if r else x for r, x in enumerate(pairs)]

    def pass_over(crosses):
        return [lax.ppermute(x, "seq", hop(half, 1, r)) for r, x in enumerate(crosses)]

    def tie(*parts):
        return lax.optimization_barrier(parts)

    gated = [gate(half, cols, (query, key, value, grad), taps) for cols in spans]
    pairs, crosses = [list(x) for x in zip(*gated, strict=True)]
    tap_specs = spectral(
        taps_kernel,
        256,
        [taps, forward],
        [((2 * length, width), f32)] * 2,
        [(length, 2, bf16), (length, 2, bf16)],
        tiny,
    )
    pairs[0], crosses[0] = pass_on(pairs[0]), pass_over(crosses[0])
    for c in range(1, len(spans)):
        crosses[c], pairs[0], crosses[0], tap_specs = tie(
            crosses[c], pairs[0], crosses[0], tap_specs
        )
        pairs[c], crosses[c] = pass_on(pairs[c]), pass_over(crosses[c])
    near = lax.ppermute(crosses[0][0][cut * block // 128 :], "dp", flip(replicas, 1))
    results, cross_results, keep, sends = [], [], [], []
    for c, cols in enumerate(spans):
        wide = cols.stop - cols.start
        outs = spectral(
            functools.partial(conv_kernel, half, replicas, cols.start),
            256,
            [*pairs[c], *crosses[c], *tap_specs, crosses[0][0], near, forward, inverse, *keep],
            [((4, block, wide), bf16)] * half
            + [((block, wide), bf16)] * half
            + [((3 * length // 2, width), f32)]
            + [((3 * length // 2, t.stop - t.start), bf16) for t in tiles(wide, 256)],
            [
                (length, 5, bf16),
                (length, 1, bf16),
                (2 * length, 5, f32),
                (2 * length, 1, f32),
                (2 * length, 8, bf16),
                (length, 5, bf16),
                (length, 3, f32),
            ],
            large if c else tiny,
            {2 * half + 6: 2 * half} if c else {},
        )
        keep, *more = outs[2 * half :]
        keep, sends = [keep], sends + more
        cross = list(outs[half : 2 * half])
        if c:
            sends, cross_results[-1] = tie(sends, cross_results[-1])
        results.append(pass_on(outs[:half]))
        cross_results.append(pass_over(cross))
    grad_filter = sum_filter(*keep, sends, length, half, replicas)
    outs = []
    for c, cols in enumerate(spans):
        outs = finish(half, cols.start, results[c], cross_results[c], grad, value, key, outs)
    return *outs, grad_filter


def solution(mesh):
    rows = P(("dp", "seq"), "chan")
    return jax.shard_map(
        functools.partial(local, mesh.shape["dp"], mesh.shape["seq"] // 2),
        mesh=mesh,
        in_specs=(rows, rows, rows, rows, P(None, ("chan", "seq"))),
        out_specs=(rows, rows, rows, P("dp", ("chan", "seq"))),
        check_vma=False,
    )
```
